32 devices in a mesh: section: 4 (over y, x), dp: 8 (over z, core).
Axes of the slice: x: 2, y: 2, z: 4, core: 2. Of those that a mesh axis runs over, the one named last changes fastest.
Arguments:
- failed: int32 [8], P('dp'), may hold values from 0 to 3
- unfinished: int32 [8, 2], P('dp'), may hold values from 0 to 7, as said below
- lengths: int32 [8, 2], P('dp'), may hold values from 1 to 64
- acts: bfloat16 [4, 16, 64, 4096], P('section', 'dp'), may hold values from -100 to 100
- out_grads: bfloat16 [4, 64, 64, 512], P('section', 'dp'), may hold values from -30 to 30
- shadow_weight: bfloat16 [4, 4096, 512], P('section'), may hold values from -0.09375 to 0.09375
- shadow_gain: bfloat16 [4, 4096], P('section'), may hold values from 0.099609375 to 1.8984375
Outputs:
- in_grad: bfloat16 [4, 16, 64, 4096], P('section', 'dp')
- gain_grad: float32 [4, 4096], P('section', 'dp')
- bias_grad: float32 [4, 512], P('section', 'dp')
The draws below stay inside these ranges and needn't reach their ends.
Inputs may be any that keep to these rules, and one draw needn't show every extreme that they name: `unfinished`: in each replica's row the 2 ids differ.
All inputs are finite; a program needn't handle non-finite values.
Results may differ from the reference program's by a relative error of at most 0.001.
Values may be sent and summed in bfloat16 or wider, within the bound.
A program may use at most 64 MiB of HBM per device.

```python
import math
import jax
import jax.numpy as jnp
from jax import lax

D = 4096
KVD = 512
MB = 2
MBALL = 8
SEQ = 64
N_SECTION = 4
N_DP = 8


def draw_failed(key, part):
    values = jax.random.randint(jax.random.fold_in(key, 5), (N_DP,), 0, N_SECTION)
    row_id = lax.broadcasted_iota(jnp.int32, (N_DP,), 0)
    values = jnp.where(row_id == 0, N_SECTION - 1, values)
    values = jnp.where(row_id == N_DP - 1, 0, values)
    return values.astype(jnp.int32)


def draw_unfinished(key, part):
    scores = jax.random.randint(key, (N_DP, MBALL), 0, 2 ** 20) * MBALL
    column = lax.broadcasted_iota(jnp.int32, (N_DP, MBALL), 1)
    row_id = lax.broadcasted_iota(jnp.int32, (N_DP, MBALL), 0)
    scores = scores + column
    scores = scores + jnp.where((row_id == 0) & (column == MBALL - 1), 2 ** 26, 0)
    scores = scores + jnp.where((row_id == N_DP - 1) & (column == 0), 2 ** 26, 0)
    order = jnp.argsort(-scores, axis=1, stable=True)
    return order[:, :MB].astype(jnp.int32)


def draw_lengths(key, part):
    values = jax.random.randint(key, (N_DP, MB), 1, SEQ + 1)
    row_id = lax.broadcasted_iota(jnp.int32, (N_DP, MB), 0)
    column = lax.broadcasted_iota(jnp.int32, (N_DP, MB), 1)
    values = jnp.where((row_id == 0) & (column == 0), SEQ, values)
    values = jnp.where((row_id == N_DP - 1) & (column == MB - 1), 1, values)
    return values.astype(jnp.int32)


def draw_acts(key, part):
    key_a, key_b, key_c = jax.random.split(jax.random.fold_in(key, 11), 3)
    shape = (N_SECTION, N_DP * MB, SEQ, D)
    base = jnp.clip(jax.random.normal(key_a, shape, jnp.float32), -4.0, 4.0)
    row_scale = jnp.exp(jax.random.uniform(key_b, (N_SECTION, N_DP * MB, SEQ, 1), jnp.float32, 0.0, math.log(10.0)))
    col_scale = jnp.exp(jax.random.uniform(key_c, (N_SECTION, 1, 1, D), jnp.float32, math.log(0.5), math.log(2.0)))
    return jnp.clip(base * row_scale * col_scale, -100.0, 100.0).astype(jnp.bfloat16)


def draw_out_grads(key, part):
    key_a = jax.random.fold_in(jax.random.fold_in(key, 23), 0)
    shape = (N_SECTION, N_DP * MBALL, SEQ, KVD)
    replica = (lax.broadcasted_iota(jnp.int32, (1, N_DP * MBALL, 1, 1), 1) // MBALL).astype(jnp.float32)
    spread_pos = replica / max(N_DP - 1, 1)
    base = jnp.clip(jax.random.normal(key_a, shape, jnp.float32), -4.0, 4.0)
    scale = jnp.exp(math.log(3.0) * spread_pos)
    return jnp.clip(base * scale, -30.0, 30.0).astype(jnp.bfloat16)


def shard_levels(key, extent, shards, low, high):
    factor_of = 1.0
    for position, parts in shards:
        steps = jax.random.uniform(jax.random.fold_in(jax.random.fold_in(key, 6), position), (parts,), jnp.float32, low / len(shards), high / len(shards))
        factor_of = factor_of * jnp.repeat(jnp.exp(steps), extent[position] // parts).reshape((-1,) + (1,) * (len(extent) - 1 - position))
    return factor_of


def noise(rng, shape, spread, bound, cuts=(), kind=jnp.bfloat16):
    values = spread * jax.random.normal(rng, shape, jnp.float32)
    if cuts:
        values = values * shard_levels(rng, shape, cuts, -0.22, 0.18)
    return jnp.clip(values, -bound, bound).astype(kind)


def setup_inputs(seed: int = 0) -> dict:
    keys = jax.random.split(jax.random.key(seed), 8)
    failed = draw_failed(jax.random.fold_in(keys[7], 71), 0)
    unfinished = draw_unfinished(jax.random.fold_in(keys[7], 71), 0)
    lengths = draw_lengths(jax.random.fold_in(keys[7], 71), 0)
    acts = draw_acts(jax.random.fold_in(keys[7], 71), 0)
    out_grads = draw_out_grads(jax.random.fold_in(keys[7], 71), 0)
    shadow_weight = noise(keys[5], (N_SECTION, D, KVD), D ** -0.5, 0.09375, ((0, 4),))
    shadow_gain = jnp.clip(1.0 + 0.18 * jax.random.normal(keys[6], (N_SECTION, D), jnp.float32), 0.099609375, 1.8984375).astype(jnp.bfloat16)
    return dict(failed=failed, unfinished=unfinished, lengths=lengths, acts=acts, out_grads=out_grads, shadow_weight=shadow_weight, shadow_gain=shadow_gain)


EPSILON = 1e-06

def reference(failed, unfinished, lengths, acts, out_grads, shadow_weight, shadow_gain):
    helper = (failed + N_SECTION - 1) % N_SECTION
    source = (failed + 1) % N_SECTION
    replica_ids = jnp.arange(N_DP, dtype=jnp.int32)

    def one_replica(rep, help_section, src_section, picked_ids, live_len):
        rows = lax.dynamic_slice_in_dim(lax.dynamic_index_in_dim(acts, help_section, 0, keepdims=False), (rep * MB).astype(jnp.int32), MB, 0).reshape(MB * SEQ, D)
        sent = lax.dynamic_slice_in_dim(lax.dynamic_index_in_dim(out_grads, src_section, 0, keepdims=False), (rep * MBALL).astype(jnp.int32), MBALL, 0)
        picked = jnp.take(sent, picked_ids, axis=0)
        live = jnp.arange(SEQ, dtype=jnp.int32)[None, :] < live_len[:, None]
        grads = jnp.where(live[..., None], picked, jnp.zeros_like(picked)).reshape(MB * SEQ, KVD)
        weight = lax.dynamic_index_in_dim(shadow_weight, help_section, 0, keepdims=False)
        gain = lax.dynamic_index_in_dim(shadow_gain, help_section, 0, keepdims=False).astype(jnp.float32)
        wide = rows.astype(jnp.float32)
        inv_rms = lax.rsqrt(lax.optimization_barrier(jnp.mean(wide * wide, axis=1, keepdims=True)) + EPSILON)
        normed = wide * inv_rms
        grad_norm = jnp.dot(grads, weight.T, preferred_element_type=jnp.float32)
        grad_hat = grad_norm * gain[None, :]
        inner = lax.optimization_barrier(jnp.mean(grad_hat * normed, axis=1, keepdims=True))
        dx = inv_rms * (grad_hat - normed * inner)
        gain_row = lax.optimization_barrier(jnp.sum(grad_norm * normed, axis=0)) / N_DP
        bias_row = lax.optimization_barrier(jnp.sum(grads.astype(jnp.float32), axis=0)) / N_DP
        return (dx.astype(jnp.bfloat16).reshape(MB, SEQ, D), gain_row, bias_row)
    dx_all, gain_rows, bias_rows = lax.map(lambda a: one_replica(*a), (replica_ids, helper, source, unfinished, lengths))
    section_ids = jnp.arange(N_SECTION, dtype=jnp.int32)
    hit = section_ids[:, None] == helper[None, :]
    dx_flat = dx_all.reshape(N_DP * MB, SEQ, D)
    hit_rows = jnp.repeat(hit, MB, axis=1)
    in_grad = jnp.where(hit_rows[:, :, None, None], dx_flat[None], jnp.zeros((), jnp.bfloat16))
    weights = hit.astype(jnp.float32)
    gain_grad = jnp.dot(weights, gain_rows, precision=lax.Precision.HIGHEST)
    bias_grad = jnp.dot(weights, bias_rows, precision=lax.Precision.HIGHEST)
    return (in_grad, gain_grad, bias_grad)
```

```python
import functools

import jax
import jax.numpy as jnp
from jax import lax
from jax.experimental import pallas as pl
from jax.experimental.pallas import tpu as pltpu
from jax.sharding import PartitionSpec as P

EPSILON = 1e-06
MESH = pl.DeviceIdType.MESH
LANES = 128
HALVES = 2
TILE = 256
ROWS = 16


def recover_kernel(
    sections,
    replicas,
    failed,
    unfinished,
    lengths,
    gain_ref,
    acts_hbm,
    out_grads_hbm,
    weight_hbm,
    dx_ref,
    share_ref,
    acts,
    out_grads,
    weight,
    send,
    recv,
    normed,
    inv_rms,
    grad_norm,
    parts_out,
    parts_in,
    load_sem,
    send_sem,
    recv_sem,
    part_send_sem,
    part_recv_sem,
):
    section = lax.axis_index("section")
    replica = lax.axis_index("dp")
    slots, seq = unfinished.shape[1], out_grads.shape[1]
    features, half = out_grads.shape[2], out_grads.shape[2] // HALVES
    rows, channels = acts.shape
    gain_share, bias_share = channels // replicas, features // replicas
    gain_chunk = max(gain_share, LANES)
    group = gain_chunk // gain_share
    chunks = channels // gain_chunk
    gain_rows = gain_chunk // LANES

    loads = [
        pltpu.make_async_copy(source, target, load_sem.at[i])
        for i, (source, target) in enumerate(
            ((out_grads_hbm, out_grads), (acts_hbm, acts), (weight_hbm, weight))
        )
    ]
    for load in loads:
        load.start()

    target = lax.rem(section + sections - 2, sections)
    origin = lax.rem(section + 2, sections)
    barrier = pltpu.get_barrier_semaphore()
    greeted = 1
    pl.semaphore_signal(barrier, inc=1, device_id={"section": origin}, device_id_type=MESH)
    if (sections - 2) % sections != 2 % sections:
        greeted = 2
        pl.semaphore_signal(barrier, inc=1, device_id={"section": target}, device_id_type=MESH)
    for step in range(1, replicas):
        peer = lax.rem(replica + step, replicas)
        pl.semaphore_signal(barrier, inc=1, device_id={"dp": peer}, device_id_type=MESH)

    is_source = lax.rem(failed[0] + 1, sections) == section
    loads[0].wait()
    for slot in range(slots):
        picked = out_grads[unfinished[0, slot]].astype(jnp.float32)
        limit = jnp.where(is_source, lengths[0, slot], 0)
        position = lax.broadcasted_iota(jnp.int32, picked.shape, 0)
        picked = jnp.where(position < limit, picked, 0.0).astype(jnp.bfloat16)
        for part in range(HALVES):
            send[part, slot * seq : (slot + 1) * seq, :] = picked[:, part * half : (part + 1) * half]

    pl.semaphore_wait(barrier, greeted + replicas - 1)
    copies = []
    for part in range(HALVES):
        copy = pltpu.make_async_remote_copy(
            src_ref=send.at[part],
            dst_ref=recv.at[part],
            send_sem=send_sem.at[part],
            recv_sem=recv_sem.at[part],
            device_id={"section": target},
            device_id_type=MESH,
        )
        copy.start()
        copies.append(copy)

    loads[1].wait()
    for block in range(rows // ROWS):
        at = slice(block * ROWS, (block + 1) * ROWS)
        wide = acts[at, :].astype(jnp.float32)
        scale = lax.rsqrt(jnp.mean(wide * wide, axis=1, keepdims=True) + EPSILON)
        inv_rms[at, :] = jnp.broadcast_to(scale, (ROWS, LANES))
        normed[at, :] = wide * scale

    loads[2].wait()
    copies[0].wait_recv()
    for tile in range(channels // TILE):
        at = slice(tile * TILE, (tile + 1) * TILE)
        grad_norm[:, at] = lax.dot_general(
            recv[0], weight[at, :half], (((1,), (1,)), ((), ())), preferred_element_type=jnp.float32
        )

    copies[1].wait_recv()
    for part in range(HALVES):
        bias = jnp.sum(recv[part].astype(jnp.float32), axis=0, keepdims=True) / replicas
        for peer in range(replicas):
            lane = (peer * bias_share // LANES) * LANES
            if part * half <= lane < (part + 1) * half:
                lane -= part * half
                parts_out[peer, gain_rows : gain_rows + 1, :] = bias[:, lane : lane + LANES]

    inner = jnp.zeros((rows, LANES), jnp.float32)
    part_copies = []
    width = min(TILE, gain_chunk)
    first = replica // group
    for step in range(1, chunks + 1):
        chunk = lax.rem(first + step, chunks)
        for piece in range(gain_chunk // width):
            at = pl.ds(pl.multiple_of(chunk * gain_chunk + piece * width, width), width)
            value = grad_norm[:, at] + lax.dot_general(
                recv[1], weight[at, half:], (((1,), (1,)), ((), ())), preferred_element_type=jnp.float32
            )
            grad_norm[:, at] = value
            product = value * normed[:, at]
            column = jnp.sum(product, axis=0, keepdims=True) / replicas
            for g in range(group):
                for row in range(width // LANES):
                    place = piece * (width // LANES) + row
                    parts_out[chunk * group + g, place : place + 1, :] = column[:, row * LANES : (row + 1) * LANES]
            product = product * gain_ref[:, at].astype(jnp.float32)
            for row in range(width // LANES):
                inner = inner + product[:, row * LANES : (row + 1) * LANES]
        for g in range(group):
            if group == 1 and step == chunks:
                continue
            peer = chunk * group + g
            copy = pltpu.make_async_remote_copy(
                src_ref=parts_out.at[peer],
                dst_ref=parts_in.at[replica],
                send_sem=part_send_sem.at[peer],
                recv_sem=part_recv_sem.at[replica],
                device_id={"dp": peer},
                device_id_type=MESH,
            )
            if group == 1:
                copy.start()
            else:
                pl.when(peer != replica)(copy.start)
    parts_in[replica] = parts_out[replica]

    inner = jnp.sum(inner, axis=1, keepdims=True) / channels
    gain = gain_ref[...].astype(jnp.float32)
    for block in range(rows // ROWS):
        at = slice(block * ROWS, (block + 1) * ROWS)
        result = inv_rms[at, :1] * (grad_norm[at, :] * gain - normed[at, :] * inner[at])
        dx_ref[at, :] = result.astype(jnp.bfloat16)

    for step in range(1, replicas):
        peer = lax.rem(replica + step, replicas)
        copy = pltpu.make_async_remote_copy(
            src_ref=parts_out.at[peer],
            dst_ref=parts_in.at[peer],
            send_sem=part_send_sem.at[peer],
            recv_sem=part_recv_sem.at[peer],
            device_id={"dp": peer},
            device_id_type=MESH,
        )
        copy.wait_recv()
        copy.wait_send()
    share_ref[...] = jnp.sum(parts_in[...], axis=0)
    for copy in copies:
        copy.wait_send()


def own_lanes(value, replica, share):
    if share >= LANES:
        return value
    options = LANES // share
    own = value[:, :share]
    for option in range(1, options):
        other = value[:, option * share : (option + 1) * share]
        own = jnp.where(lax.rem(replica, options) == option, other, own)
    return own


def write_kernel(dx, share, in_grad, gain_grad, bias_grad, sem):
    copy = pltpu.make_async_copy(dx, in_grad, sem)
    copy.start()
    replica = lax.axis_index("dp")
    gain_share, bias_share = gain_grad.shape[1], bias_grad.shape[1]
    gain_rows = max(gain_share, LANES) // LANES
    if gain_rows == 1:
        gain_grad[...] = own_lanes(share[:1, :], replica, gain_share)
    else:
        for row in range(gain_rows):
            gain_grad[:, row * LANES : (row + 1) * LANES] = share[row : row + 1, :]
    bias_grad[...] = own_lanes(share[gain_rows : gain_rows + 1, :], replica, bias_share)
    copy.wait()


def per_device(failed, unfinished, lengths, acts, out_grads, shadow_weight, shadow_gain):
    sections = lax.axis_size("section")
    replicas = lax.axis_size("dp")
    slots, seq, channels = acts.shape[1:]
    features = out_grads.shape[3]
    rows = slots * seq
    gain_rows = max(channels // replicas, LANES) // LANES
    packed = -(-(gain_rows + 1) // 8) * 8
    f32, bf16 = jnp.float32, jnp.bfloat16
    smem = pl.BlockSpec(memory_space=pltpu.SMEM)
    vmem = pl.BlockSpec(memory_space=pltpu.VMEM)
    hbm = pl.BlockSpec(memory_space=pltpu.HBM)
    dx, share = pl.pallas_call(
        functools.partial(recover_kernel, sections, replicas),
        out_shape=(
            pltpu.VMEM((rows, channels), bf16),
            pltpu.VMEM((packed, LANES), f32),
        ),
        in_specs=[smem, smem, smem, vmem, hbm, hbm, hbm],
        out_specs=(vmem, vmem),
        scratch_shapes=[
            pltpu.VMEM((rows, channels), bf16),
            pltpu.VMEM(out_grads.shape[1:], bf16),
            pltpu.VMEM((channels, features), bf16),
            pltpu.VMEM((HALVES, rows, features // HALVES), bf16),
            pltpu.VMEM((HALVES, rows, features // HALVES), bf16),
            pltpu.VMEM((rows, channels), f32),
            pltpu.VMEM((rows, LANES), f32),
            pltpu.VMEM((rows, channels), f32),
            pltpu.VMEM((replicas, packed, LANES), f32),
            pltpu.VMEM((replicas, packed, LANES), f32),
            pltpu.SemaphoreType.DMA((3,)),
            pltpu.SemaphoreType.DMA((HALVES,)),
            pltpu.SemaphoreType.DMA((HALVES,)),
            pltpu.SemaphoreType.DMA((replicas,)),
            pltpu.SemaphoreType.DMA((replicas,)),
        ],
        compiler_params=pltpu.CompilerParams(
            collective_id=0, has_side_effects=True, vmem_limit_bytes=28 * 2**20
        ),
        cost_estimate=pl.CostEstimate(
            flops=2 * rows * features * channels,
            bytes_accessed=2 * (channels * features + 2 * rows * channels),
            transcendentals=rows,
        ),
        name="recover",
    )(
        failed,
        unfinished,
        lengths,
        shadow_gain,
        *(
            pltpu.with_memory_space_constraint(operand, pltpu.HBM)
            for operand in (acts.reshape(rows, channels), out_grads[0], shadow_weight[0])
        ),
    )
    in_grad, gain_grad, bias_grad = pl.pallas_call(
        write_kernel,
        out_shape=(
            jax.ShapeDtypeStruct((rows, channels), bf16),
            jax.ShapeDtypeStruct((1, channels // replicas), f32),
            jax.ShapeDtypeStruct((1, features // replicas), f32),
        ),
        in_specs=[vmem, vmem],
        out_specs=(hbm, vmem, vmem),
        scratch_shapes=[pltpu.SemaphoreType.DMA],
        compiler_params=pltpu.CompilerParams(vmem_limit_bytes=8 * 2**20),
        cost_estimate=pl.CostEstimate(
            flops=0, bytes_accessed=4 * rows * channels, transcendentals=0
        ),
        name="write",
    )(dx, share)
    return in_grad.reshape(1, slots, seq, channels), gain_grad, bias_grad


def solution(mesh):
    in_specs = (
        P("dp"),
        P("dp", None),
        P("dp", None),
        P("section", "dp", None, None),
        P("section", "dp", None, None),
        P("section", None, None),
        P("section", None),
    )
    out_specs = (P("section", "dp", None, None), P("section", "dp"), P("section", "dp"))
    return jax.shard_map(
        per_device, mesh=mesh, in_specs=in_specs, out_specs=out_specs, check_vma=False
    )
```

```python
import functools

import jax
import jax.numpy as jnp
from jax import lax
from jax.experimental import pallas as pl
from jax.experimental.pallas import tpu as pltpu
from jax.sharding import PartitionSpec as P

EPSILON = 1e-06
MESH = pl.DeviceIdType.MESH
LANES = 128
HALVES = 2
TILE = 256
ROWS = 16
PIECES = 4


def recover_kernel(
    sections,
    replicas,
    failed,
    unfinished_hbm,
    lengths_hbm,
    gain_hbm,
    acts_hbm,
    out_grads_hbm,
    weight_hbm,
    dx_ref,
    share_ref,
    unfinished,
    lengths,
    gain_ref,
    acts,
    out_grads,
    weight,
    send,
    recv,
    normed,
    inv_rms,
    grad_norm,
    parts_out,
    parts_in,
    load_sem,
    send_sem,
    recv_sem,
    part_send_sem,
    part_recv_sem,
):
    section = lax.axis_index("section")
    replica = lax.axis_index("dp")
    slots, seq = unfinished.shape[1], out_grads.shape[1]
    features, half = out_grads.shape[2], out_grads.shape[2] // HALVES
    rows, channels = acts.shape
    gain_share, bias_share = channels // replicas, features // replicas
    gain_chunk = max(gain_share, LANES)
    group = gain_chunk // gain_share
    chunks = channels // gain_chunk
    gain_rows = gain_chunk // LANES

    loads = [
        pltpu.make_async_copy(source, target, load_sem.at[i])
        for i, (source, target) in enumerate(
            (
                (unfinished_hbm, unfinished),
                (lengths_hbm, lengths),
                (out_grads_hbm, out_grads),
                (acts_hbm, acts),
                (gain_hbm, gain_ref),
                (weight_hbm, weight),
            )
        )
    ]
    target = lax.rem(section + sections - 2, sections)
    origin = lax.rem(section + 2, sections)
    barrier = pltpu.get_barrier_semaphore()
    greeted = 1
    pl.semaphore_signal(barrier, inc=1, device_id={"section": origin}, device_id_type=MESH)
    if (sections - 2) % sections != 2 % sections:
        greeted = 2
        pl.semaphore_signal(barrier, inc=1, device_id={"section": target}, device_id_type=MESH)
    for step in range(1, replicas):
        peer = lax.rem(replica + step, replicas)
        pl.semaphore_signal(barrier, inc=1, device_id={"dp": peer}, device_id_type=MESH)

    for load in loads[:4]:
        load.start()
    for load in loads[:3]:
        load.wait()
    for load in loads[4:]:
        load.start()
    is_source = lax.rem(failed[0] + 1, sections) == section
    for slot in range(slots):
        picked = out_grads[unfinished[0, slot]].astype(jnp.float32)
        limit = jnp.where(is_source, lengths[0, slot], 0)
        position = lax.broadcasted_iota(jnp.int32, picked.shape, 0)
        picked = jnp.where(position < limit, picked, 0.0).astype(jnp.bfloat16)
        for part in range(HALVES):
            send[part, slot * seq : (slot + 1) * seq, :] = picked[:, part * half : (part + 1) * half]

    pl.semaphore_wait(barrier, greeted + replicas - 1)
    copies = []
    for part in range(HALVES):
        copy = pltpu.make_async_remote_copy(
            src_ref=send.at[part],
            dst_ref=recv.at[part],
            send_sem=send_sem.at[part],
            recv_sem=recv_sem.at[part],
            device_id={"section": target},
            device_id_type=MESH,
        )
        copy.start()
        copies.append(copy)

    loads[3].wait()
    for block in range(rows // ROWS):
        at = slice(block * ROWS, (block + 1) * ROWS)
        wide = acts[at, :].astype(jnp.float32)
        scale = lax.rsqrt(jnp.mean(wide * wide, axis=1, keepdims=True) + EPSILON)
        inv_rms[at, :] = jnp.broadcast_to(scale, (ROWS, LANES))
        normed[at, :] = wide * scale

    loads[4].wait()
    loads[5].wait()
    copies[0].wait_recv()
    for tile in range(channels // TILE):
        at = slice(tile * TILE, (tile + 1) * TILE)
        grad_norm[:, at] = lax.dot_general(
            recv[0], weight[at, :half], (((1,), (1,)), ((), ())), preferred_element_type=jnp.float32
        )

    copies[1].wait_recv()
    for part in range(HALVES):
        bias = jnp.sum(recv[part].astype(jnp.float32), axis=0, keepdims=True) / replicas
        for peer in range(replicas):
            lane = (peer * bias_share // LANES) * LANES
            if part * half <= lane < (part + 1) * half:
                lane -= part * half
                parts_out[peer, gain_rows : gain_rows + 1, :] = bias[:, lane : lane + LANES]

    inner = jnp.zeros((rows, LANES), jnp.float32)
    part_copies = []
    width = min(TILE, gain_chunk)
    first = replica // group
    for step in range(1, chunks + 1):
        chunk = lax.rem(first + step, chunks)
        for piece in range(gain_chunk // width):
            at = pl.ds(pl.multiple_of(chunk * gain_chunk + piece * width, width), width)
            value = grad_norm[:, at] + lax.dot_general(
                recv[1], weight[at, half:], (((1,), (1,)), ((), ())), preferred_element_type=jnp.float32
            )
            grad_norm[:, at] = value
            product = value * normed[:, at]
            column = jnp.sum(product, axis=0, keepdims=True) / replicas
            for g in range(group):
                for row in range(width // LANES):
                    place = piece * (width // LANES) + row
                    parts_out[chunk * group + g, place : place + 1, :] = column[:, row * LANES : (row + 1) * LANES]
            product = product * gain_ref[:, at].astype(jnp.float32)
            for row in range(width // LANES):
                inner = inner + product[:, row * LANES : (row + 1) * LANES]
        for g in range(group):
            if group == 1 and step == chunks:
                continue
            peer = chunk * group + g
            copy = pltpu.make_async_remote_copy(
                src_ref=parts_out.at[peer],
                dst_ref=parts_in.at[replica],
                send_sem=part_send_sem.at[peer],
                recv_sem=part_recv_sem.at[replica],
                device_id={"dp": peer},
                device_id_type=MESH,
            )
            if group == 1:
                copy.start()
            else:
                pl.when(peer != replica)(copy.start)
    parts_in[replica] = parts_out[replica]

    inner = jnp.sum(inner, axis=1, keepdims=True) / channels
    gain = gain_ref[...].astype(jnp.float32)
    for block in range(rows // ROWS):
        at = slice(block * ROWS, (block + 1) * ROWS)
        result = inv_rms[at, :1] * (grad_norm[at, :] * gain - normed[at, :] * inner[at])
        dx_ref[at, :] = result.astype(jnp.bfloat16)

    for step in range(1, replicas):
        peer = lax.rem(replica + step, replicas)
        copy = pltpu.make_async_remote_copy(
            src_ref=parts_out.at[peer],
            dst_ref=parts_in.at[peer],
            send_sem=part_send_sem.at[peer],
            recv_sem=part_recv_sem.at[peer],
            device_id={"dp": peer},
            device_id_type=MESH,
        )
        copy.wait_recv()
        copy.wait_send()
    share_ref[...] = jnp.sum(parts_in[...], axis=0)
    for copy in copies:
        copy.wait_send()


def own_lanes(value, replica, share):
    if share >= LANES:
        return value
    options = LANES // share
    own = value[:, :share]
    for option in range(1, options):
        other = value[:, option * share : (option + 1) * share]
        own = jnp.where(lax.rem(replica, options) == option, other, own)
    return own


def write_kernel(dx, share, in_grad, gain_grad, bias_grad, gain, bias, sem):
    rows = dx.shape[0]
    copies = []
    for i in range(PIECES):
        at = pl.ds(i * (rows // PIECES), rows // PIECES)
        copies.append(pltpu.make_async_copy(dx.at[at], in_grad.at[at], sem.at[i]))
        copies[-1].start()
    replica = lax.axis_index("dp")
    gain_share, bias_share = gain.shape[1], bias.shape[1]
    gain_rows = max(gain_share, LANES) // LANES
    if gain_rows == 1:
        gain[...] = own_lanes(share[:1, :], replica, gain_share)
    else:
        for row in range(gain_rows):
            gain[:, row * LANES : (row + 1) * LANES] = share[row : row + 1, :]
    bias[...] = own_lanes(share[gain_rows : gain_rows + 1, :], replica, bias_share)
    for i, (source, target) in enumerate(((gain, gain_grad), (bias, bias_grad))):
        copies.append(pltpu.make_async_copy(source, target, sem.at[PIECES + i]))
        copies[-1].start()
    for copy in copies:
        copy.wait()


def per_device(failed, unfinished, lengths, acts, out_grads, shadow_weight, shadow_gain):
    sections = lax.axis_size("section")
    replicas = lax.axis_size("dp")
    slots, seq, channels = acts.shape[1:]
    features = out_grads.shape[3]
    rows = slots * seq
    gain_rows = max(channels // replicas, LANES) // LANES
    packed = -(-(gain_rows + 1) // 8) * 8
    f32, bf16 = jnp.float32, jnp.bfloat16
    vmem = pl.BlockSpec(memory_space=pltpu.VMEM)
    hbm = pl.BlockSpec(memory_space=pltpu.HBM)
    dx, share = pl.pallas_call(
        functools.partial(recover_kernel, sections, replicas),
        out_shape=(
            pltpu.VMEM((rows, channels), bf16),
            pltpu.VMEM((packed, LANES), f32),
        ),
        in_specs=[pl.BlockSpec(memory_space=pltpu.SMEM)] + [hbm] * 6,
        out_specs=(vmem, vmem),
        scratch_shapes=[
            pltpu.SMEM(unfinished.shape, jnp.int32),
            pltpu.SMEM(lengths.shape, jnp.int32),
            pltpu.VMEM(shadow_gain.shape, bf16),
            pltpu.VMEM((rows, channels), bf16),
            pltpu.VMEM(out_grads.shape[1:], bf16),
            pltpu.VMEM((channels, features), bf16),
            pltpu.VMEM((HALVES, rows, features // HALVES), bf16),
            pltpu.VMEM((HALVES, rows, features // HALVES), bf16),
            pltpu.VMEM((rows, channels), f32),
            pltpu.VMEM((rows, LANES), f32),
            pltpu.VMEM((rows, channels), f32),
            pltpu.VMEM((replicas, packed, LANES), f32),
            pltpu.VMEM((replicas, packed, LANES), f32),
            pltpu.SemaphoreType.DMA((6,)),
            pltpu.SemaphoreType.DMA((HALVES,)),
            pltpu.SemaphoreType.DMA((HALVES,)),
            pltpu.SemaphoreType.DMA((replicas,)),
            pltpu.SemaphoreType.DMA((replicas,)),
        ],
        compiler_params=pltpu.CompilerParams(
            collective_id=0, has_side_effects=True, vmem_limit_bytes=28 * 2**20
        ),
        cost_estimate=pl.CostEstimate(
            flops=2 * rows * features * channels,
            bytes_accessed=2 * (channels * features + 2 * rows * channels),
            transcendentals=rows,
        ),
        name="recover",
    )(
        failed,
        *(
            pltpu.with_memory_space_constraint(operand, pltpu.HBM)
            for operand in (
                unfinished,
                lengths,
                shadow_gain,
                acts.reshape(rows, channels),
                out_grads[0],
                shadow_weight[0],
            )
        ),
    )
    in_grad, gain_grad, bias_grad = pl.pallas_call(
        write_kernel,
        out_shape=(
            jax.ShapeDtypeStruct((rows, channels), bf16),
            jax.ShapeDtypeStruct((1, channels // replicas), f32),
            jax.ShapeDtypeStruct((1, features // replicas), f32),
        ),
        in_specs=[vmem, vmem],
        out_specs=(hbm, hbm, hbm),
        scratch_shapes=[
            pltpu.VMEM((1, channels // replicas), f32),
            pltpu.VMEM((1, features // replicas), f32),
            pltpu.SemaphoreType.DMA((PIECES + 2,)),
        ],
        compiler_params=pltpu.CompilerParams(vmem_limit_bytes=8 * 2**20),
        cost_estimate=pl.CostEstimate(
            flops=0, bytes_accessed=4 * rows * channels, transcendentals=0
        ),
        name="write",
    )(dx, share)
    return in_grad.reshape(1, slots, seq, channels), gain_grad, bias_grad


def solution(mesh):
    in_specs = (
        P("dp"),
        P("dp", None),
        P("dp", None),
        P("section", "dp", None, None),
        P("section", "dp", None, None),
        P("section", None, None),
        P("section", None),
    )
    out_specs = (P("section", "dp", None, None), P("section", "dp"), P("section", "dp"))
    return jax.shard_map(
        per_device, mesh=mesh, in_specs=in_specs, out_specs=out_specs, check_vma=False
    )
```

```python
import functools

import jax
import jax.numpy as jnp
from jax import lax
from jax.experimental import pallas as pl
from jax.experimental.pallas import tpu as pltpu
from jax.sharding import PartitionSpec as P

EPSILON = 1e-06
MESH = pl.DeviceIdType.MESH
LANES = 128
HALVES = 2
TILE = 256
ROWS = 16
PIECES = 4


def recover_kernel(
    sections,
    replicas,
    failed,
    unfinished_hbm,
    lengths_hbm,
    gain_hbm,
    acts_hbm,
    out_grads_hbm,
    weight_hbm,
    dx_ref,
    share_ref,
    unfinished,
    lengths,
    gain_ref,
    acts,
    out_grads,
    weight,
    send,
    recv,
    normed,
    inv_rms,
    grad_norm,
    parts_out,
    parts_in,
    load_sem,
    send_sem,
    recv_sem,
    part_send_sem,
    part_recv_sem,
):
    section = lax.axis_index("section")
    replica = lax.axis_index("dp")
    slots, seq = unfinished.shape[1], out_grads.shape[1]
    features, half = out_grads.shape[2], out_grads.shape[2] // HALVES
    rows, channels = acts.shape
    gain_share, bias_share = channels // replicas, features // replicas
    gain_chunk = max(gain_share, LANES)
    group = gain_chunk // gain_share
    chunks = channels // gain_chunk
    gain_rows = gain_chunk // LANES

    def load(source, target, pieces, start):
        size = source.shape[0] // pieces
        return [
            pltpu.make_async_copy(
                source.at[pl.ds(i * size, size)], target.at[pl.ds(i * size, size)], load_sem.at[start + i]
            )
            for i in range(pieces)
        ]

    small = load(unfinished_hbm, unfinished, 1, 0) + load(lengths_hbm, lengths, 1, 1)
    load_gain = load(gain_hbm, gain_ref, 1, 2)
    load_grads = load(out_grads_hbm, out_grads, PIECES, 3)
    load_acts = load(acts_hbm, acts, PIECES, 3 + PIECES)
    load_weight = load(weight_hbm, weight, PIECES, 3 + 2 * PIECES)

    def add_bias(part):
        bias = jnp.sum(recv[part].astype(jnp.float32), axis=0, keepdims=True) / replicas
        for peer in range(replicas):
            lane = (peer * bias_share // LANES) * LANES
            if part * half <= lane < (part + 1) * half:
                lane -= part * half
                parts_out[peer, gain_rows : gain_rows + 1, :] = bias[:, lane : lane + LANES]

    target = lax.rem(section + sections - 2, sections)
    origin = lax.rem(section + 2, sections)
    barrier = pltpu.get_barrier_semaphore()
    greeted = 1
    pl.semaphore_signal(barrier, inc=1, device_id={"section": origin}, device_id_type=MESH)
    if (sections - 2) % sections != 2 % sections:
        greeted = 2
        pl.semaphore_signal(barrier, inc=1, device_id={"section": target}, device_id_type=MESH)
    for step in range(1, replicas):
        peer = lax.rem(replica + step, replicas)
        pl.semaphore_signal(barrier, inc=1, device_id={"dp": peer}, device_id_type=MESH)

    for copy in small + load_grads:
        copy.start()
    for copy in small + load_grads:
        copy.wait()
    for copy in load_acts + load_weight + load_gain:
        copy.start()
    is_source = lax.rem(failed[0] + 1, sections) == section
    for slot in range(slots):
        picked = out_grads[unfinished[0, slot]].astype(jnp.float32)
        limit = jnp.where(is_source, lengths[0, slot], 0)
        position = lax.broadcasted_iota(jnp.int32, picked.shape, 0)
        picked = jnp.where(position < limit, picked, 0.0).astype(jnp.bfloat16)
        for part in range(HALVES):
            send[part, slot * seq : (slot + 1) * seq, :] = picked[:, part * half : (part + 1) * half]

    pl.semaphore_wait(barrier, greeted + replicas - 1)
    copies = []
    for part in range(HALVES):
        copy = pltpu.make_async_remote_copy(
            src_ref=send.at[part],
            dst_ref=recv.at[part],
            send_sem=send_sem.at[part],
            recv_sem=recv_sem.at[part],
            device_id={"section": target},
            device_id_type=MESH,
        )
        copy.start()
        copies.append(copy)

    for copy in load_acts:
        copy.wait()
    for block in range(rows // ROWS):
        at = slice(block * ROWS, (block + 1) * ROWS)
        wide = acts[at, :].astype(jnp.float32)
        scale = lax.rsqrt(jnp.mean(wide * wide, axis=1, keepdims=True) + EPSILON)
        inv_rms[at, :] = jnp.broadcast_to(scale, (ROWS, LANES))
        normed[at, :] = wide * scale

    for copy in load_gain + load_weight:
        copy.wait()
    copies[0].wait_recv()
    for tile in range(channels // TILE):
        at = slice(tile * TILE, (tile + 1) * TILE)
        grad_norm[:, at] = lax.dot_general(
            recv[0], weight[at, :half], (((1,), (1,)), ((), ())), preferred_element_type=jnp.float32
        )

    add_bias(0)
    copies[1].wait_recv()
    add_bias(1)

    inner = jnp.zeros((rows, LANES), jnp.float32)
    part_copies = []
    width = min(TILE, gain_chunk)
    first = replica // group
    for step in range(1, chunks + 1):
        chunk = lax.rem(first + step, chunks)
        for piece in range(gain_chunk // width):
            at = pl.ds(pl.multiple_of(chunk * gain_chunk + piece * width, width), width)
            value = grad_norm[:, at] + lax.dot_general(
                recv[1], weight[at, half:], (((1,), (1,)), ((), ())), preferred_element_type=jnp.float32
            )
            grad_norm[:, at] = value
            product = value * normed[:, at]
            column = jnp.sum(product, axis=0, keepdims=True) / replicas
            for g in range(group):
                for row in range(width // LANES):
                    place = piece * (width // LANES) + row
                    parts_out[chunk * group + g, place : place + 1, :] = column[:, row * LANES : (row + 1) * LANES]
            product = product * gain_ref[:, at].astype(jnp.float32)
            for row in range(width // LANES):
                inner = inner + product[:, row * LANES : (row + 1) * LANES]
        for g in range(group):
            if group == 1 and step == chunks:
                continue
            peer = chunk * group + g
            copy = pltpu.make_async_remote_copy(
                src_ref=parts_out.at[peer],
                dst_ref=parts_in.at[replica],
                send_sem=part_send_sem.at[peer],
                recv_sem=part_recv_sem.at[replica],
                device_id={"dp": peer},
                device_id_type=MESH,
            )
            if group == 1:
                copy.start()
            else:
                pl.when(peer != replica)(copy.start)
    parts_in[replica] = parts_out[replica]

    inner = jnp.sum(inner, axis=1, keepdims=True) / channels
    gain = gain_ref[...].astype(jnp.float32)
    for block in range(rows // ROWS):
        at = slice(block * ROWS, (block + 1) * ROWS)
        result = inv_rms[at, :1] * (grad_norm[at, :] * gain - normed[at, :] * inner[at])
        dx_ref[at, :] = result.astype(jnp.bfloat16)

    for step in range(1, replicas):
        peer = lax.rem(replica + step, replicas)
        copy = pltpu.make_async_remote_copy(
            src_ref=parts_out.at[peer],
            dst_ref=parts_in.at[peer],
            send_sem=part_send_sem.at[peer],
            recv_sem=part_recv_sem.at[peer],
            device_id={"dp": peer},
            device_id_type=MESH,
        )
        copy.wait_recv()
        copy.wait_send()
    share_ref[...] = jnp.sum(parts_in[...], axis=0)
    for copy in copies:
        copy.wait_send()


def own_lanes(value, replica, share):
    if share >= LANES:
        return value
    options = LANES // share
    own = value[:, :share]
    for option in range(1, options):
        other = value[:, option * share : (option + 1) * share]
        own = jnp.where(lax.rem(replica, options) == option, other, own)
    return own


def write_kernel(dx, share, in_grad, gain_grad, bias_grad, gain, bias, sem):
    rows = dx.shape[0]
    copies = []
    for i in range(PIECES):
        at = pl.ds(i * (rows // PIECES), rows // PIECES)
        copies.append(pltpu.make_async_copy(dx.at[at], in_grad.at[at], sem.at[i]))
        copies[-1].start()
    replica = lax.axis_index("dp")
    gain_share, bias_share = gain.shape[1], bias.shape[1]
    gain_rows = max(gain_share, LANES) // LANES
    if gain_rows == 1:
        gain[...] = own_lanes(share[:1, :], replica, gain_share)
    else:
        for row in range(gain_rows):
            gain[:, row * LANES : (row + 1) * LANES] = share[row : row + 1, :]
    bias[...] = own_lanes(share[gain_rows : gain_rows + 1, :], replica, bias_share)
    for i, (source, target) in enumerate(((gain, gain_grad), (bias, bias_grad))):
        copies.append(pltpu.make_async_copy(source, target, sem.at[PIECES + i]))
        copies[-1].start()
    for copy in copies:
        copy.wait()


def per_device(failed, unfinished, lengths, acts, out_grads, shadow_weight, shadow_gain):
    sections = lax.axis_size("section")
    replicas = lax.axis_size("dp")
    slots, seq, channels = acts.shape[1:]
    features = out_grads.shape[3]
    rows = slots * seq
    gain_rows = max(channels // replicas, LANES) // LANES
    packed = -(-(gain_rows + 1) // 8) * 8
    f32, bf16 = jnp.float32, jnp.bfloat16
    vmem = pl.BlockSpec(memory_space=pltpu.VMEM)
    hbm = pl.BlockSpec(memory_space=pltpu.HBM)
    dx, share = pl.pallas_call(
        functools.partial(recover_kernel, sections, replicas),
        out_shape=(
            pltpu.VMEM((rows, channels), bf16),
            pltpu.VMEM((packed, LANES), f32),
        ),
        in_specs=[pl.BlockSpec(memory_space=pltpu.SMEM)] + [hbm] * 6,
        out_specs=(vmem, vmem),
        scratch_shapes=[
            pltpu.SMEM(unfinished.shape, jnp.int32),
            pltpu.SMEM(lengths.shape, jnp.int32),
            pltpu.VMEM(shadow_gain.shape, bf16),
            pltpu.VMEM((rows, channels), bf16),
            pltpu.VMEM(out_grads.shape[1:], bf16),
            pltpu.VMEM((channels, features), bf16),
            pltpu.VMEM((HALVES, rows, features // HALVES), bf16),
            pltpu.VMEM((HALVES, rows, features // HALVES), bf16),
            pltpu.VMEM((rows, channels), f32),
            pltpu.VMEM((rows, LANES), f32),
            pltpu.VMEM((rows, channels), f32),
            pltpu.VMEM((replicas, packed, LANES), f32),
            pltpu.VMEM((replicas, packed, LANES), f32),
            pltpu.SemaphoreType.DMA((3 + 3 * PIECES,)),
            pltpu.SemaphoreType.DMA((HALVES,)),
            pltpu.SemaphoreType.DMA((HALVES,)),
            pltpu.SemaphoreType.DMA((replicas,)),
            pltpu.SemaphoreType.DMA((replicas,)),
        ],
        compiler_params=pltpu.CompilerParams(
            collective_id=0, has_side_effects=True, vmem_limit_bytes=28 * 2**20
        ),
        cost_estimate=pl.CostEstimate(
            flops=2 * rows * features * channels,
            bytes_accessed=2 * (channels * features + 2 * rows * channels),
            transcendentals=rows,
        ),
        name="recover",
    )(
        failed,
        *(
            pltpu.with_memory_space_constraint(operand, pltpu.HBM)
            for operand in (
                unfinished,
                lengths,
                shadow_gain,
                acts.reshape(rows, channels),
                out_grads[0],
                shadow_weight[0],
            )
        ),
    )
    in_grad, gain_grad, bias_grad = pl.pallas_call(
        write_kernel,
        out_shape=(
            jax.ShapeDtypeStruct((rows, channels), bf16),
            jax.ShapeDtypeStruct((1, channels // replicas), f32),
            jax.ShapeDtypeStruct((1, features // replicas), f32),
        ),
        in_specs=[vmem, vmem],
        out_specs=(hbm, hbm, hbm),
        scratch_shapes=[
            pltpu.VMEM((1, channels // replicas), f32),
            pltpu.VMEM((1, features // replicas), f32),
            pltpu.SemaphoreType.DMA((PIECES + 2,)),
        ],
        compiler_params=pltpu.CompilerParams(vmem_limit_bytes=8 * 2**20),
        cost_estimate=pl.CostEstimate(
            flops=0, bytes_accessed=4 * rows * channels, transcendentals=0
        ),
        name="write",
    )(dx, share)
    return in_grad.reshape(1, slots, seq, channels), gain_grad, bias_grad


def solution(mesh):
    in_specs = (
        P("dp"),
        P("dp", None),
        P("dp", None),
        P("section", "dp", None, None),
        P("section", "dp", None, None),
        P("section", None, None),
        P("section", None),
    )
    out_specs = (P("section", "dp", None, None), P("section", "dp"), P("section", "dp"))
    return jax.shard_map(
        per_device, mesh=mesh, in_specs=in_specs, out_specs=out_specs, check_vma=False
    )
```

```python
import functools

import jax
import jax.numpy as jnp
from jax import lax
from jax.experimental import pallas as pl
from jax.experimental.pallas import tpu as pltpu
from jax.sharding import PartitionSpec as P

EPSILON = 1e-06
MESH = pl.DeviceIdType.MESH
LANES = 128
HALVES = 2
TILE = 256
ROWS = 16
PIECES = 4


def recover_kernel(
    sections,
    replicas,
    failed,
    unfinished_hbm,
    lengths_hbm,
    gain_hbm,
    acts_hbm,
    out_grads_hbm,
    weight_hbm,
    dx_ref,
    share_ref,
    unfinished,
    lengths,
    gain_ref,
    acts,
    out_grads,
    weight,
    send,
    recv,
    normed,
    inv_rms,
    totals,
    grad_norm,
    parts_out,
    parts_in,
    load_sem,
    send_sem,
    recv_sem,
    part_send_sem,
    part_recv_sem,
):
    section = lax.axis_index("section")
    replica = lax.axis_index("dp")
    slots, seq = unfinished.shape[1], out_grads.shape[1]
    features, half = out_grads.shape[2], out_grads.shape[2] // HALVES
    rows, channels = acts.shape
    gain_share, bias_share = channels // replicas, features // replicas
    gain_chunk = max(gain_share, LANES)
    group = gain_chunk // gain_share
    chunks = channels // gain_chunk
    gain_rows = gain_chunk // LANES

    def load(source, target, pieces, start):
        size = source.shape[0] // pieces
        return [
            pltpu.make_async_copy(
                source.at[pl.ds(i * size, size)], target.at[pl.ds(i * size, size)], load_sem.at[start + i]
            )
            for i in range(pieces)
        ]

    small = load(unfinished_hbm, unfinished, 1, 0) + load(lengths_hbm, lengths, 1, 1)
    load_gain = load(gain_hbm, gain_ref, 1, 2)
    load_grads = load(out_grads_hbm, out_grads, PIECES, 3)
    load_acts = load(acts_hbm, acts, PIECES, 3 + PIECES)
    load_weight = load(weight_hbm, weight, PIECES, 3 + 2 * PIECES)

    def add_bias(part):
        bias = jnp.sum(recv[part].astype(jnp.float32), axis=0, keepdims=True) / replicas
        for peer in range(replicas):
            lane = (peer * bias_share // LANES) * LANES
            if part * half <= lane < (part + 1) * half:
                lane -= part * half
                parts_out[peer, gain_rows : gain_rows + 1, :] = bias[:, lane : lane + LANES]

    target = lax.rem(section + sections - 2, sections)
    origin = lax.rem(section + 2, sections)
    barrier = pltpu.get_barrier_semaphore()
    greeted = 1
    pl.semaphore_signal(barrier, inc=1, device_id={"section": origin}, device_id_type=MESH)
    if (sections - 2) % sections != 2 % sections:
        greeted = 2
        pl.semaphore_signal(barrier, inc=1, device_id={"section": target}, device_id_type=MESH)
    for step in range(1, replicas):
        peer = lax.rem(replica + step, replicas)
        pl.semaphore_signal(barrier, inc=1, device_id={"dp": peer}, device_id_type=MESH)

    for copy in small + load_grads:
        copy.start()
    for copy in small + load_grads:
        copy.wait()
    for copy in load_acts + load_weight + load_gain:
        copy.start()
    is_source = lax.rem(failed[0] + 1, sections) == section
    for slot in range(slots):
        picked = out_grads[unfinished[0, slot]].astype(jnp.float32)
        limit = jnp.where(is_source, lengths[0, slot], 0)
        position = lax.broadcasted_iota(jnp.int32, picked.shape, 0)
        picked = jnp.where(position < limit, picked, 0.0).astype(jnp.bfloat16)
        for part in range(HALVES):
            send[part, slot * seq : (slot + 1) * seq, :] = picked[:, part * half : (part + 1) * half]

    pl.semaphore_wait(barrier, greeted + replicas - 1)
    copies = []
    for part in range(HALVES):
        copy = pltpu.make_async_remote_copy(
            src_ref=send.at[part],
            dst_ref=recv.at[part],
            send_sem=send_sem.at[part],
            recv_sem=recv_sem.at[part],
            device_id={"section": target},
            device_id_type=MESH,
        )
        copy.start()
        copies.append(copy)

    for copy in load_acts:
        copy.wait()
    def normalize(block, carry):
        at = pl.ds(pl.multiple_of(block * ROWS, ROWS), ROWS)
        wide = acts[at, :].astype(jnp.float32)
        scale = lax.rsqrt(jnp.mean(wide * wide, axis=1, keepdims=True) + EPSILON)
        inv_rms[at, :] = jnp.broadcast_to(scale, (ROWS, LANES))
        normed[at, :] = wide * scale
        return carry

    lax.fori_loop(0, rows // ROWS, normalize, 0)
    for copy in load_gain + load_weight:
        copy.wait()
    copies[0].wait_recv()

    def multiply(tile, carry):
        at = pl.ds(pl.multiple_of(tile * 2 * TILE, 2 * TILE), 2 * TILE)
        grad_norm[:, at] = lax.dot_general(
            recv[0], weight[at, :half], (((1,), (1,)), ((), ())), preferred_element_type=jnp.float32
        )
        return carry

    lax.fori_loop(0, channels // (2 * TILE), multiply, 0)

    add_bias(0)
    copies[1].wait_recv()
    add_bias(1)

    width = min(TILE, gain_chunk)
    first = replica // group

    def finish(step, inner):
        chunk = lax.rem(first + step, chunks)
        for piece in range(gain_chunk // width):
            at = pl.ds(pl.multiple_of(chunk * gain_chunk + piece * width, width), width)
            value = grad_norm[:, at] + lax.dot_general(
                recv[1], weight[at, half:], (((1,), (1,)), ((), ())), preferred_element_type=jnp.float32
            )
            grad_norm[:, at] = value
            product = value * normed[:, at]
            column = jnp.sum(product, axis=0, keepdims=True) / replicas
            for g in range(group):
                for row in range(width // LANES):
                    place = piece * (width // LANES) + row
                    parts_out[chunk * group + g, place : place + 1, :] = column[:, row * LANES : (row + 1) * LANES]
            product = product * gain_ref[:, at].astype(jnp.float32)
            for row in range(width // LANES):
                inner = inner + product[:, row * LANES : (row + 1) * LANES]
        for g in range(group):
            peer = chunk * group + g

            @pl.when(peer != replica)
            def _():
                pltpu.make_async_remote_copy(
                    src_ref=parts_out.at[peer],
                    dst_ref=parts_in.at[replica],
                    send_sem=part_send_sem.at[peer],
                    recv_sem=part_recv_sem.at[replica],
                    device_id={"dp": peer},
                    device_id_type=MESH,
                ).start()

        return inner

    inner = lax.fori_loop(1, chunks + 1, finish, jnp.zeros((rows, LANES), jnp.float32))
    parts_in[replica] = parts_out[replica]

    totals[...] = jnp.broadcast_to(jnp.sum(inner, axis=1, keepdims=True) / channels, totals.shape)
    gain = gain_ref[...].astype(jnp.float32)

    def correct(block, carry):
        at = pl.ds(pl.multiple_of(block * ROWS, ROWS), ROWS)
        result = inv_rms[at, :1] * (grad_norm[at, :] * gain - normed[at, :] * totals[at, :1])
        dx_ref[at, :] = result.astype(jnp.bfloat16)
        return carry

    lax.fori_loop(0, rows // ROWS, correct, 0)

    for step in range(1, replicas):
        peer = lax.rem(replica + step, replicas)
        copy = pltpu.make_async_remote_copy(
            src_ref=parts_out.at[peer],
            dst_ref=parts_in.at[peer],
            send_sem=part_send_sem.at[peer],
            recv_sem=part_recv_sem.at[peer],
            device_id={"dp": peer},
            device_id_type=MESH,
        )
        copy.wait_recv()
        copy.wait_send()
    share_ref[...] = jnp.sum(parts_in[...], axis=0)
    for copy in copies:
        copy.wait_send()


def own_lanes(value, replica, share):
    if share >= LANES:
        return value
    options = LANES // share
    own = value[:, :share]
    for option in range(1, options):
        other = value[:, option * share : (option + 1) * share]
        own = jnp.where(lax.rem(replica, options) == option, other, own)
    return own


def write_kernel(dx, share, in_grad, gain_grad, bias_grad, gain, bias, sem):
    rows = dx.shape[0]
    copies = []
    for i in range(PIECES):
        at = pl.ds(i * (rows // PIECES), rows // PIECES)
        copies.append(pltpu.make_async_copy(dx.at[at], in_grad.at[at], sem.at[i]))
        copies[-1].start()
    replica = lax.axis_index("dp")
    gain_share, bias_share = gain.shape[1], bias.shape[1]
    gain_rows = max(gain_share, LANES) // LANES
    if gain_rows == 1:
        gain[...] = own_lanes(share[:1, :], replica, gain_share)
    else:
        for row in range(gain_rows):
            gain[:, row * LANES : (row + 1) * LANES] = share[row : row + 1, :]
    bias[...] = own_lanes(share[gain_rows : gain_rows + 1, :], replica, bias_share)
    for i, (source, target) in enumerate(((gain, gain_grad), (bias, bias_grad))):
        copies.append(pltpu.make_async_copy(source, target, sem.at[PIECES + i]))
        copies[-1].start()
    for copy in copies:
        copy.wait()


def per_device(failed, unfinished, lengths, acts, out_grads, shadow_weight, shadow_gain):
    sections = lax.axis_size("section")
    replicas = lax.axis_size("dp")
    slots, seq, channels = acts.shape[1:]
    features = out_grads.shape[3]
    rows = slots * seq
    gain_rows = max(channels // replicas, LANES) // LANES
    packed = -(-(gain_rows + 1) // 8) * 8
    f32, bf16 = jnp.float32, jnp.bfloat16
    vmem = pl.BlockSpec(memory_space=pltpu.VMEM)
    hbm = pl.BlockSpec(memory_space=pltpu.HBM)
    dx, share = pl.pallas_call(
        functools.partial(recover_kernel, sections, replicas),
        out_shape=(
            pltpu.VMEM((rows, channels), bf16),
            pltpu.VMEM((packed, LANES), f32),
        ),
        in_specs=[pl.BlockSpec(memory_space=pltpu.SMEM)] + [hbm] * 6,
        out_specs=(vmem, vmem),
        scratch_shapes=[
            pltpu.SMEM(unfinished.shape, jnp.int32),
            pltpu.SMEM(lengths.shape, jnp.int32),
            pltpu.VMEM(shadow_gain.shape, bf16),
            pltpu.VMEM((rows, channels), bf16),
            pltpu.VMEM(out_grads.shape[1:], bf16),
            pltpu.VMEM((channels, features), bf16),
            pltpu.VMEM((HALVES, rows, features // HALVES), bf16),
            pltpu.VMEM((HALVES, rows, features // HALVES), bf16),
            pltpu.VMEM((rows, channels), f32),
            pltpu.VMEM((rows, LANES), f32),
            pltpu.VMEM((rows, LANES), f32),
            pltpu.VMEM((rows, channels), f32),
            pltpu.VMEM((replicas, packed, LANES), f32),
            pltpu.VMEM((replicas, packed, LANES), f32),
            pltpu.SemaphoreType.DMA((3 + 3 * PIECES,)),
            pltpu.SemaphoreType.DMA((HALVES,)),
            pltpu.SemaphoreType.DMA((HALVES,)),
            pltpu.SemaphoreType.DMA((replicas,)),
            pltpu.SemaphoreType.DMA((replicas,)),
        ],
        compiler_params=pltpu.CompilerParams(
            collective_id=0, has_side_effects=True, vmem_limit_bytes=28 * 2**20
        ),
        cost_estimate=pl.CostEstimate(
            flops=2 * rows * features * channels,
            bytes_accessed=2 * (channels * features + 2 * rows * channels),
            transcendentals=rows,
        ),
        name="recover",
    )(
        failed,
        *(
            pltpu.with_memory_space_constraint(operand, pltpu.HBM)
            for operand in (
                unfinished,
                lengths,
                shadow_gain,
                acts.reshape(rows, channels),
                out_grads[0],
                shadow_weight[0],
            )
        ),
    )
    in_grad, gain_grad, bias_grad = pl.pallas_call(
        write_kernel,
        out_shape=(
            jax.ShapeDtypeStruct((rows, channels), bf16),
            jax.ShapeDtypeStruct((1, channels // replicas), f32),
            jax.ShapeDtypeStruct((1, features // replicas), f32),
        ),
        in_specs=[vmem, vmem],
        out_specs=(hbm, hbm, hbm),
        scratch_shapes=[
            pltpu.VMEM((1, channels // replicas), f32),
            pltpu.VMEM((1, features // replicas), f32),
            pltpu.SemaphoreType.DMA((PIECES + 2,)),
        ],
        compiler_params=pltpu.CompilerParams(vmem_limit_bytes=8 * 2**20),
        cost_estimate=pl.CostEstimate(
            flops=0, bytes_accessed=4 * rows * channels, transcendentals=0
        ),
        name="write",
    )(dx, share)
    return in_grad.reshape(1, slots, seq, channels), gain_grad, bias_grad


def solution(mesh):
    in_specs = (
        P("dp"),
        P("dp", None),
        P("dp", None),
        P("section", "dp", None, None),
        P("section", "dp", None, None),
        P("section", None, None),
        P("section", None),
    )
    out_specs = (P("section", "dp", None, None), P("section", "dp"), P("section", "dp"))
    return jax.shard_map(
        per_device, mesh=mesh, in_specs=in_specs, out_specs=out_specs, check_vma=False
    )
```

```python
import functools

import jax
import jax.numpy as jnp
from jax import lax
from jax.experimental import pallas as pl
from jax.experimental.pallas import tpu as pltpu
from jax.sharding import PartitionSpec as P

EPSILON = 1e-06
MESH = pl.DeviceIdType.MESH
LANES = 128
HALVES = 2
TILE = 256
ROWS = 16
PIECES = 4


def recover_kernel(
    sections,
    replicas,
    failed,
    unfinished_hbm,
    lengths_hbm,
    gain_hbm,
    acts_hbm,
    out_grads_hbm,
    weight_hbm,
    dx_ref,
    share_ref,
    unfinished,
    lengths,
    gain_ref,
    acts,
    out_grads,
    weight,
    turned,
    send,
    recv,
    normed,
    inv_rms,
    grad_norm,
    parts_out,
    parts_in,
    load_sem,
    send_sem,
    recv_sem,
    part_send_sem,
    part_recv_sem,
):
    section = lax.axis_index("section")
    replica = lax.axis_index("dp")
    slots, seq = unfinished.shape[1], out_grads.shape[1]
    features, half = out_grads.shape[2], out_grads.shape[2] // HALVES
    rows, channels = acts.shape
    gain_share, bias_share = channels // replicas, features // replicas
    gain_chunk = max(gain_share, LANES)
    group = gain_chunk // gain_share
    chunks = channels // gain_chunk
    gain_rows = gain_chunk // LANES

    def load(source, target, pieces, start):
        size = source.shape[0] // pieces
        return [
            pltpu.make_async_copy(
                source.at[pl.ds(i * size, size)], target.at[pl.ds(i * size, size)], load_sem.at[start + i]
            )
            for i in range(pieces)
        ]

    small = load(unfinished_hbm, unfinished, 1, 0) + load(lengths_hbm, lengths, 1, 1)
    load_gain = load(gain_hbm, gain_ref, 1, 2)
    load_grads = load(out_grads_hbm, out_grads, PIECES, 3)
    load_acts = load(acts_hbm, acts, PIECES, 3 + PIECES)
    load_weight = load(weight_hbm, weight, PIECES, 3 + 2 * PIECES)

    def add_bias(part):
        bias = jnp.sum(recv[part].astype(jnp.float32), axis=0, keepdims=True) / replicas
        for peer in range(replicas):
            lane = (peer * bias_share // LANES) * LANES
            if part * half <= lane < (part + 1) * half:
                lane -= part * half
                parts_out[peer, gain_rows : gain_rows + 1, :] = bias[:, lane : lane + LANES]

    target = lax.rem(section + sections - 2, sections)
    origin = lax.rem(section + 2, sections)
    barrier = pltpu.get_barrier_semaphore()
    greeted = 1
    pl.semaphore_signal(barrier, inc=1, device_id={"section": origin}, device_id_type=MESH)
    if (sections - 2) % sections != 2 % sections:
        greeted = 2
        pl.semaphore_signal(barrier, inc=1, device_id={"section": target}, device_id_type=MESH)
    for step in range(1, replicas):
        peer = lax.rem(replica + step, replicas)
        pl.semaphore_signal(barrier, inc=1, device_id={"dp": peer}, device_id_type=MESH)

    for copy in small + load_grads:
        copy.start()
    for copy in small + load_grads:
        copy.wait()
    for copy in load_acts + load_weight + load_gain:
        copy.start()
    is_source = lax.rem(failed[0] + 1, sections) == section
    copies = []
    for part in range(HALVES):
        for slot in range(slots):
            picked = out_grads[unfinished[0, slot], :, part * half : (part + 1) * half].astype(jnp.float32)
            limit = jnp.where(is_source, lengths[0, slot], 0)
            position = lax.broadcasted_iota(jnp.int32, picked.shape, 0)
            picked = jnp.where(position < limit, picked, 0.0).astype(jnp.bfloat16)
            send[part, slot * seq : (slot + 1) * seq, :] = picked
        if part == 0:
            pl.semaphore_wait(barrier, greeted + replicas - 1)
        copy = pltpu.make_async_remote_copy(
            src_ref=send.at[part],
            dst_ref=recv.at[part],
            send_sem=send_sem.at[part],
            recv_sem=recv_sem.at[part],
            device_id={"section": target},
            device_id_type=MESH,
        )
        copy.start()
        copies.append(copy)

    for copy in load_acts:
        copy.wait()
    for block in range(rows // ROWS):
        at = slice(block * ROWS, (block + 1) * ROWS)
        wide = acts[at, :].astype(jnp.float32)
        scale = lax.rsqrt(jnp.mean(wide * wide, axis=1, keepdims=True) + EPSILON)
        inv_rms[at, :] = jnp.broadcast_to(scale, (ROWS, LANES))
        normed[at, :] = wide * scale

    for copy in load_gain + load_weight:
        copy.wait()
    for tile in range(channels // TILE):
        at = slice(tile * TILE, (tile + 1) * TILE)
        turned[:, at] = weight[at, half:].T
    copies[0].wait_recv()
    for tile in range(channels // TILE):
        at = slice(tile * TILE, (tile + 1) * TILE)
        grad_norm[:, at] = lax.dot_general(
            recv[0], weight[at, :half], (((1,), (1,)), ((), ())), preferred_element_type=jnp.float32
        )

    add_bias(0)
    copies[1].wait_recv()
    add_bias(1)

    inner = jnp.zeros((rows, LANES), jnp.float32)
    part_copies = []
    width = min(TILE, gain_chunk)
    first = replica // group
    for step in range(1, chunks + 1):
        chunk = lax.rem(first + step, chunks)
        for piece in range(gain_chunk // width):
            at = pl.ds(pl.multiple_of(chunk * gain_chunk + piece * width, width), width)
            value = grad_norm[:, at] + lax.dot_general(
                recv[1], turned[:, at], (((1,), (0,)), ((), ())), preferred_element_type=jnp.float32
            )
            grad_norm[:, at] = value
            product = value * normed[:, at]
            column = jnp.sum(product, axis=0, keepdims=True) / replicas
            for g in range(group):
                for row in range(width // LANES):
                    place = piece * (width // LANES) + row
                    parts_out[chunk * group + g, place : place + 1, :] = column[:, row * LANES : (row + 1) * LANES]
            product = product * gain_ref[:, at].astype(jnp.float32)
            for row in range(width // LANES):
                inner = inner + product[:, row * LANES : (row + 1) * LANES]
        for g in range(group):
            if group == 1 and step == chunks:
                continue
            peer = chunk * group + g
            copy = pltpu.make_async_remote_copy(
                src_ref=parts_out.at[peer],
                dst_ref=parts_in.at[replica],
                send_sem=part_send_sem.at[peer],
                recv_sem=part_recv_sem.at[replica],
                device_id={"dp": peer},
                device_id_type=MESH,
            )
            if group == 1:
                copy.start()
            else:
                pl.when(peer != replica)(copy.start)
    parts_in[replica] = parts_out[replica]

    inner = jnp.sum(inner, axis=1, keepdims=True) / channels
    gain = gain_ref[...].astype(jnp.float32)
    for block in range(rows // ROWS):
        at = slice(block * ROWS, (block + 1) * ROWS)
        result = inv_rms[at, :1] * (grad_norm[at, :] * gain - normed[at, :] * inner[at])
        dx_ref[at, :] = result.astype(jnp.bfloat16)

    for step in range(1, replicas):
        peer = lax.rem(replica + step, replicas)
        copy = pltpu.make_async_remote_copy(
            src_ref=parts_out.at[peer],
            dst_ref=parts_in.at[peer],
            send_sem=part_send_sem.at[peer],
            recv_sem=part_recv_sem.at[peer],
            device_id={"dp": peer},
            device_id_type=MESH,
        )
        copy.wait_recv()
        copy.wait_send()
    share_ref[...] = jnp.sum(parts_in[...], axis=0)
    for copy in copies:
        copy.wait_send()


def own_lanes(value, replica, share):
    if share >= LANES:
        return value
    options = LANES // share
    own = value[:, :share]
    for option in range(1, options):
        other = value[:, option * share : (option + 1) * share]
        own = jnp.where(lax.rem(replica, options) == option, other, own)
    return own


def write_kernel(dx, share, in_grad, gain_grad, bias_grad, gain, bias, sem):
    rows = dx.shape[0]
    copies = []
    for i in range(PIECES):
        at = pl.ds(i * (rows // PIECES), rows // PIECES)
        copies.append(pltpu.make_async_copy(dx.at[at], in_grad.at[at], sem.at[i]))
        copies[-1].start()
    replica = lax.axis_index("dp")
    gain_share, bias_share = gain.shape[1], bias.shape[1]
    gain_rows = max(gain_share, LANES) // LANES
    if gain_rows == 1:
        gain[...] = own_lanes(share[:1, :], replica, gain_share)
    else:
        for row in range(gain_rows):
            gain[:, row * LANES : (row + 1) * LANES] = share[row : row + 1, :]
    bias[...] = own_lanes(share[gain_rows : gain_rows + 1, :], replica, bias_share)
    for i, (source, target) in enumerate(((gain, gain_grad), (bias, bias_grad))):
        copies.append(pltpu.make_async_copy(source, target, sem.at[PIECES + i]))
        copies[-1].start()
    for copy in copies:
        copy.wait()


def per_device(failed, unfinished, lengths, acts, out_grads, shadow_weight, shadow_gain):
    sections = lax.axis_size("section")
    replicas = lax.axis_size("dp")
    slots, seq, channels = acts.shape[1:]
    features = out_grads.shape[3]
    rows = slots * seq
    gain_rows = max(channels // replicas, LANES) // LANES
    packed = -(-(gain_rows + 1) // 8) * 8
    f32, bf16 = jnp.float32, jnp.bfloat16
    vmem = pl.BlockSpec(memory_space=pltpu.VMEM)
    hbm = pl.BlockSpec(memory_space=pltpu.HBM)
    dx, share = pl.pallas_call(
        functools.partial(recover_kernel, sections, replicas),
        out_shape=(
            pltpu.VMEM((rows, channels), bf16),
            pltpu.VMEM((packed, LANES), f32),
        ),
        in_specs=[pl.BlockSpec(memory_space=pltpu.SMEM)] + [hbm] * 6,
        out_specs=(vmem, vmem),
        scratch_shapes=[
            pltpu.SMEM(unfinished.shape, jnp.int32),
            pltpu.SMEM(lengths.shape, jnp.int32),
            pltpu.VMEM(shadow_gain.shape, bf16),
            pltpu.VMEM((rows, channels), bf16),
            pltpu.VMEM(out_grads.shape[1:], bf16),
            pltpu.VMEM((channels, features), bf16),
            pltpu.VMEM((features // HALVES, channels), bf16),
            pltpu.VMEM((HALVES, rows, features // HALVES), bf16),
            pltpu.VMEM((HALVES, rows, features // HALVES), bf16),
            pltpu.VMEM((rows, channels), f32),
            pltpu.VMEM((rows, LANES), f32),
            pltpu.VMEM((rows, channels), f32),
            pltpu.VMEM((replicas, packed, LANES), f32),
            pltpu.VMEM((replicas, packed, LANES), f32),
            pltpu.SemaphoreType.DMA((3 + 3 * PIECES,)),
            pltpu.SemaphoreType.DMA((HALVES,)),
            pltpu.SemaphoreType.DMA((HALVES,)),
            pltpu.SemaphoreType.DMA((replicas,)),
            pltpu.SemaphoreType.DMA((replicas,)),
        ],
        compiler_params=pltpu.CompilerParams(
            collective_id=0, has_side_effects=True, vmem_limit_bytes=28 * 2**20
        ),
        cost_estimate=pl.CostEstimate(
            flops=2 * rows * features * channels,
            bytes_accessed=2 * (channels * features + 2 * rows * channels),
            transcendentals=rows,
        ),
        name="recover",
    )(
        failed,
        *(
            pltpu.with_memory_space_constraint(operand, pltpu.HBM)
            for operand in (
                unfinished,
                lengths,
                shadow_gain,
                acts.reshape(rows, channels),
                out_grads[0],
                shadow_weight[0],
            )
        ),
    )
    in_grad, gain_grad, bias_grad = pl.pallas_call(
        write_kernel,
        out_shape=(
            jax.ShapeDtypeStruct((rows, channels), bf16),
            jax.ShapeDtypeStruct((1, channels // replicas), f32),
            jax.ShapeDtypeStruct((1, features // replicas), f32),
        ),
        in_specs=[vmem, vmem],
        out_specs=(hbm, hbm, hbm),
        scratch_shapes=[
            pltpu.VMEM((1, channels // replicas), f32),
            pltpu.VMEM((1, features // replicas), f32),
            pltpu.SemaphoreType.DMA((PIECES + 2,)),
        ],
        compiler_params=pltpu.CompilerParams(vmem_limit_bytes=8 * 2**20),
        cost_estimate=pl.CostEstimate(
            flops=0, bytes_accessed=4 * rows * channels, transcendentals=0
        ),
        name="write",
    )(dx, share)
    return in_grad.reshape(1, slots, seq, channels), gain_grad, bias_grad


def solution(mesh):
    in_specs = (
        P("dp"),
        P("dp", None),
        P("dp", None),
        P("section", "dp", None, None),
        P("section", "dp", None, None),
        P("section", None, None),
        P("section", None),
    )
    out_specs = (P("section", "dp", None, None), P("section", "dp"), P("section", "dp"))
    return jax.shard_map(
        per_device, mesh=mesh, in_specs=in_specs, out_specs=out_specs, check_vma=False
    )
```

```python
import functools

import jax
import jax.numpy as jnp
from jax import lax
from jax.experimental import pallas as pl
from jax.experimental.pallas import tpu as pltpu
from jax.sharding import PartitionSpec as P

EPSILON = 1e-06
MESH = pl.DeviceIdType.MESH
LANES = 128
HALVES = 2
TILE = 256
ROWS = 16
PIECES = 4


def recover_kernel(
    sections,
    replicas,
    failed,
    unfinished_hbm,
    lengths_hbm,
    gain_hbm,
    acts_hbm,
    out_grads_hbm,
    weight_hbm,
    dx_ref,
    share_ref,
    unfinished,
    lengths,
    gain_ref,
    acts,
    out_grads,
    weight,
    turned,
    send,
    recv,
    normed,
    inv_rms,
    grad_norm,
    parts_out,
    parts_in,
    load_sem,
    send_sem,
    recv_sem,
    part_send_sem,
    part_recv_sem,
    round_sem,
):
    section = lax.axis_index("section")
    replica = lax.axis_index("dp")
    slots, seq = unfinished.shape[1], out_grads.shape[1]
    features, half = out_grads.shape[2], out_grads.shape[2] // HALVES
    rows, channels = acts.shape
    gain_share, bias_share = channels // replicas, features // replicas
    gain_chunk = max(gain_share, LANES)
    group = gain_chunk // gain_share
    chunks = channels // gain_chunk
    gain_rows = gain_chunk // LANES

    def load(source, target, pieces, start):
        size = source.shape[0] // pieces
        return [
            pltpu.make_async_copy(
                source.at[pl.ds(i * size, size)], target.at[pl.ds(i * size, size)], load_sem.at[start + i]
            )
            for i in range(pieces)
        ]

    small = load(unfinished_hbm, unfinished, 1, 0) + load(lengths_hbm, lengths, 1, 1)
    load_gain = load(gain_hbm, gain_ref, 1, 2)
    load_grads = load(out_grads_hbm, out_grads, PIECES, 3)
    load_acts = load(acts_hbm, acts, PIECES, 3 + PIECES)
    load_weight = load(weight_hbm, weight, PIECES, 3 + 2 * PIECES)

    def add_bias(part):
        bias = jnp.sum(recv[part].astype(jnp.float32), axis=0, keepdims=True) / replicas
        for peer in range(replicas):
            lane = (peer * bias_share // LANES) * LANES
            if part * half <= lane < (part + 1) * half:
                lane -= part * half
                parts_out[peer, gain_rows : gain_rows + 1, :] = bias[:, lane : lane + LANES]

    target = lax.rem(section + sections - 2, sections)
    origin = lax.rem(section + 2, sections)
    barrier = pltpu.get_barrier_semaphore()
    greeted = 1
    pl.semaphore_signal(barrier, inc=1, device_id={"section": origin}, device_id_type=MESH)
    if (sections - 2) % sections != 2 % sections:
        greeted = 2
        pl.semaphore_signal(barrier, inc=1, device_id={"section": target}, device_id_type=MESH)
    has_below, has_above = replica >= 2, replica + 2 < replicas
    mate = replica + 1 - 2 * lax.rem(replica, 2)
    near = has_below.astype(jnp.int32) + has_above.astype(jnp.int32)
    rounds = replicas // 2 - 1

    def tell_neighbours(semaphore):
        @pl.when(has_below)
        def _():
            pl.semaphore_signal(semaphore, inc=1, device_id={"dp": replica - 2}, device_id_type=MESH)

        @pl.when(has_above)
        def _():
            pl.semaphore_signal(semaphore, inc=1, device_id={"dp": replica + 2}, device_id_type=MESH)

    def wait_round(i):
        pl.semaphore_wait(round_sem.at[i], near)
        if i + 1 < rounds:
            tell_neighbours(round_sem.at[i + 1])

    pl.semaphore_signal(barrier, inc=1, device_id={"dp": mate}, device_id_type=MESH)
    tell_neighbours(barrier)

    for copy in small + load_grads:
        copy.start()
    for copy in small + load_grads:
        copy.wait()
    for copy in load_acts + load_weight + load_gain:
        copy.start()
    is_source = lax.rem(failed[0] + 1, sections) == section
    copies = []
    for part in range(HALVES):
        for slot in range(slots):
            picked = out_grads[unfinished[0, slot], :, part * half : (part + 1) * half].astype(jnp.float32)
            limit = jnp.where(is_source, lengths[0, slot], 0)
            position = lax.broadcasted_iota(jnp.int32, picked.shape, 0)
            picked = jnp.where(position < limit, picked, 0.0).astype(jnp.bfloat16)
            send[part, slot * seq : (slot + 1) * seq, :] = picked
        if part == 0:
            pl.semaphore_wait(barrier, greeted + 1 + near)
        copy = pltpu.make_async_remote_copy(
            src_ref=send.at[part],
            dst_ref=recv.at[part],
            send_sem=send_sem.at[part],
            recv_sem=recv_sem.at[part],
            device_id={"section": target},
            device_id_type=MESH,
        )
        copy.start()
        copies.append(copy)
    if rounds > 0:
        tell_neighbours(round_sem.at[0])

    for copy in load_acts:
        copy.wait()
    for block in range(rows // ROWS):
        at = slice(block * ROWS, (block + 1) * ROWS)
        wide = acts[at, :].astype(jnp.float32)
        scale = lax.rsqrt(jnp.mean(wide * wide, axis=1, keepdims=True) + EPSILON)
        inv_rms[at, :] = jnp.broadcast_to(scale, (ROWS, LANES))
        normed[at, :] = wide * scale

    if rounds > 1:
        wait_round(0)
    for copy in load_gain + load_weight:
        copy.wait()
    for tile in range(channels // TILE):
        at = slice(tile * TILE, (tile + 1) * TILE)
        turned[:, at] = weight[at, half:].T
    if rounds > 2:
        wait_round(1)
    copies[0].wait_recv()
    for tile in range(channels // TILE):
        at = slice(tile * TILE, (tile + 1) * TILE)
        grad_norm[:, at] = lax.dot_general(
            recv[0], weight[at, :half], (((1,), (1,)), ((), ())), preferred_element_type=jnp.float32
        )

    add_bias(0)
    copies[1].wait_recv()
    add_bias(1)
    for i in range(min(2, max(rounds - 1, 0)), rounds):
        wait_round(i)

    inner = jnp.zeros((rows, LANES), jnp.float32)
    part_copies = []
    width = min(TILE, gain_chunk)
    first = replica // group
    for step in range(1, chunks + 1):
        chunk = lax.rem(first + step, chunks)
        for piece in range(gain_chunk // width):
            at = pl.ds(pl.multiple_of(chunk * gain_chunk + piece * width, width), width)
            value = grad_norm[:, at] + lax.dot_general(
                recv[1], turned[:, at], (((1,), (0,)), ((), ())), preferred_element_type=jnp.float32
            )
            grad_norm[:, at] = value
            product = value * normed[:, at]
            column = jnp.sum(product, axis=0, keepdims=True) / replicas
            for g in range(group):
                for row in range(width // LANES):
                    place = piece * (width // LANES) + row
                    parts_out[chunk * group + g, place : place + 1, :] = column[:, row * LANES : (row + 1) * LANES]
            product = product * gain_ref[:, at].astype(jnp.float32)
            for row in range(width // LANES):
                inner = inner + product[:, row * LANES : (row + 1) * LANES]
        for g in range(group):
            if group == 1 and step == chunks:
                continue
            peer = chunk * group + g
            copy = pltpu.make_async_remote_copy(
                src_ref=parts_out.at[peer],
                dst_ref=parts_in.at[replica],
                send_sem=part_send_sem.at[peer],
                recv_sem=part_recv_sem.at[replica],
                device_id={"dp": peer},
                device_id_type=MESH,
            )
            if group == 1:
                copy.start()
            else:
                pl.when(peer != replica)(copy.start)
    parts_in[replica] = parts_out[replica]

    inner = jnp.sum(inner, axis=1, keepdims=True) / channels
    gain = gain_ref[...].astype(jnp.float32)
    for block in range(rows // ROWS):
        at = slice(block * ROWS, (block + 1) * ROWS)
        result = inv_rms[at, :1] * (grad_norm[at, :] * gain - normed[at, :] * inner[at])
        dx_ref[at, :] = result.astype(jnp.bfloat16)

    for step in range(1, replicas):
        peer = lax.rem(replica + step, replicas)
        copy = pltpu.make_async_remote_copy(
            src_ref=parts_out.at[peer],
            dst_ref=parts_in.at[peer],
            send_sem=part_send_sem.at[peer],
            recv_sem=part_recv_sem.at[peer],
            device_id={"dp": peer},
            device_id_type=MESH,
        )
        copy.wait_recv()
        copy.wait_send()
    share_ref[...] = jnp.sum(parts_in[...], axis=0)
    for copy in copies:
        copy.wait_send()


def own_lanes(value, replica, share):
    if share >= LANES:
        return value
    options = LANES // share
    own = value[:, :share]
    for option in range(1, options):
        other = value[:, option * share : (option + 1) * share]
        own = jnp.where(lax.rem(replica, options) == option, other, own)
    return own


def write_kernel(dx, share, in_grad, gain_grad, bias_grad, gain, bias, sem):
    rows = dx.shape[0]
    copies = []
    for i in range(PIECES):
        at = pl.ds(i * (rows // PIECES), rows // PIECES)
        copies.append(pltpu.make_async_copy(dx.at[at], in_grad.at[at], sem.at[i]))
        copies[-1].start()
    replica = lax.axis_index("dp")
    gain_share, bias_share = gain.shape[1], bias.shape[1]
    gain_rows = max(gain_share, LANES) // LANES
    if gain_rows == 1:
        gain[...] = own_lanes(share[:1, :], replica, gain_share)
    else:
        for row in range(gain_rows):
            gain[:, row * LANES : (row + 1) * LANES] = share[row : row + 1, :]
    bias[...] = own_lanes(share[gain_rows : gain_rows + 1, :], replica, bias_share)
    for i, (source, target) in enumerate(((gain, gain_grad), (bias, bias_grad))):
        copies.append(pltpu.make_async_copy(source, target, sem.at[PIECES + i]))
        copies[-1].start()
    for copy in copies:
        copy.wait()


def per_device(failed, unfinished, lengths, acts, out_grads, shadow_weight, shadow_gain):
    sections = lax.axis_size("section")
    replicas = lax.axis_size("dp")
    slots, seq, channels = acts.shape[1:]
    features = out_grads.shape[3]
    rows = slots * seq
    gain_rows = max(channels // replicas, LANES) // LANES
    packed = -(-(gain_rows + 1) // 8) * 8
    f32, bf16 = jnp.float32, jnp.bfloat16
    vmem = pl.BlockSpec(memory_space=pltpu.VMEM)
    hbm = pl.BlockSpec(memory_space=pltpu.HBM)
    dx, share = pl.pallas_call(
        functools.partial(recover_kernel, sections, replicas),
        out_shape=(
            pltpu.VMEM((rows, channels), bf16),
            pltpu.VMEM((packed, LANES), f32),
        ),
        in_specs=[pl.BlockSpec(memory_space=pltpu.SMEM)] + [hbm] * 6,
        out_specs=(vmem, vmem),
        scratch_shapes=[
            pltpu.SMEM(unfinished.shape, jnp.int32),
            pltpu.SMEM(lengths.shape, jnp.int32),
            pltpu.VMEM(shadow_gain.shape, bf16),
            pltpu.VMEM((rows, channels), bf16),
            pltpu.VMEM(out_grads.shape[1:], bf16),
            pltpu.VMEM((channels, features), bf16),
            pltpu.VMEM((features // HALVES, channels), bf16),
            pltpu.VMEM((HALVES, rows, features // HALVES), bf16),
            pltpu.VMEM((HALVES, rows, features // HALVES), bf16),
            pltpu.VMEM((rows, channels), f32),
            pltpu.VMEM((rows, LANES), f32),
            pltpu.VMEM((rows, channels), f32),
            pltpu.VMEM((replicas, packed, LANES), f32),
            pltpu.VMEM((replicas, packed, LANES), f32),
            pltpu.SemaphoreType.DMA((3 + 3 * PIECES,)),
            pltpu.SemaphoreType.DMA((HALVES,)),
            pltpu.SemaphoreType.DMA((HALVES,)),
            pltpu.SemaphoreType.DMA((replicas,)),
            pltpu.SemaphoreType.DMA((replicas,)),
            pltpu.SemaphoreType.REGULAR((max(replicas // 2 - 1, 1),)),
        ],
        compiler_params=pltpu.CompilerParams(
            collective_id=0, has_side_effects=True, vmem_limit_bytes=28 * 2**20
        ),
        cost_estimate=pl.CostEstimate(
            flops=2 * rows * features * channels,
            bytes_accessed=2 * (channels * features + 2 * rows * channels),
            transcendentals=rows,
        ),
        name="recover",
    )(
        failed,
        *(
            pltpu.with_memory_space_constraint(operand, pltpu.HBM)
            for operand in (
                unfinished,
                lengths,
                shadow_gain,
                acts.reshape(rows, channels),
                out_grads[0],
                shadow_weight[0],
            )
        ),
    )
    in_grad, gain_grad, bias_grad = pl.pallas_call(
        write_kernel,
        out_shape=(
            jax.ShapeDtypeStruct((rows, channels), bf16),
            jax.ShapeDtypeStruct((1, channels // replicas), f32),
            jax.ShapeDtypeStruct((1, features // replicas), f32),
        ),
        in_specs=[vmem, vmem],
        out_specs=(hbm, hbm, hbm),
        scratch_shapes=[
            pltpu.VMEM((1, channels // replicas), f32),
            pltpu.VMEM((1, features // replicas), f32),
            pltpu.SemaphoreType.DMA((PIECES + 2,)),
        ],
        compiler_params=pltpu.CompilerParams(vmem_limit_bytes=8 * 2**20),
        cost_estimate=pl.CostEstimate(
            flops=0, bytes_accessed=4 * rows * channels, transcendentals=0
        ),
        name="write",
    )(dx, share)
    return in_grad.reshape(1, slots, seq, channels), gain_grad, bias_grad


def solution(mesh):
    in_specs = (
        P("dp"),
        P("dp", None),
        P("dp", None),
        P("section", "dp", None, None),
        P("section", "dp", None, None),
        P("section", None, None),
        P("section", None),
    )
    out_specs = (P("section", "dp", None, None), P("section", "dp"), P("section", "dp"))
    return jax.shard_map(
        per_device, mesh=mesh, in_specs=in_specs, out_specs=out_specs, check_vma=False
    )
```
